1024 devices in a mesh: grp: 32 (over z, core), bal: 32 (over x, y).
Axes of the slice: x: 4, y: 8, z: 16, core: 2. Of those that a mesh axis runs over, the one named last changes fastest.
Arguments:
- tokens: bfloat16 [262144, 1024], P(('grp', 'bal')), may hold values from -6 to 6
- cotangent: bfloat16 [262144, 1024], P(('grp', 'bal')), may hold values from -6 to 6
- w_in: bfloat16 [1024, 2048], replicated, may hold values from -0.1875 to 0.1875
- w_out: bfloat16 [512, 1024], replicated, may hold values from -0.25 to 0.25
- lengths: int32 [32, 32, 2], replicated, may hold values from 64 to 192, as said below
- page_place: int32 [32, 32, 32], replicated, may hold values from 0 to 31, each once within a row
Outputs:
- output: bfloat16 [262144, 1024], P(('grp', 'bal'))
- grad_tokens: bfloat16 [262144, 1024], P(('grp', 'bal'))
- weight_grad: bfloat16 [512, 1024], replicated
The draws below stay inside these ranges and needn't reach their ends.
Inputs may be any that keep to these rules, and one draw needn't show every extreme that they name: For every g and r, lengths[g, r, 0] + lengths[g, r, 1] = 256; in every group some entry equals 192. For every g and r, page_place[g, r] is a permutation of 0 .. 31.
All inputs are finite; a program needn't handle non-finite values.
Results may differ from the reference program's by a relative error of at most 0.014.
Values may be sent and summed in bfloat16 or wider, within the bound.
A program may use at most 64 MiB of HBM per device.

```python
import math
import jax
import jax.numpy as jnp
from jax import lax

D = 1024
HEADS = 4
MINLEN = 64
RB = 256
E = 512
CAP = 192
ROWS = 262144
N_GRP = 32
N_BAL = 32


def draw_lengths(key, part):
    key = jax.random.fold_in(key, 11)
    key_first, key_forced, key_flip = jax.random.split(key, 3)
    first_len = jax.random.randint(key_first, (N_GRP, N_BAL), MINLEN, CAP + 1)
    forced = jax.random.randint(key_forced, (N_GRP, 1), 0, N_BAL)
    first_len = jnp.where(jnp.arange(N_BAL)[None, :] == forced, CAP, first_len)
    other_len = RB - first_len
    flip_bits = jax.random.randint(key_flip, (N_GRP, N_BAL), 0, 2)
    lead_len = jnp.where(flip_bits == 1, other_len, first_len)
    tail_len = jnp.where(flip_bits == 1, first_len, other_len)
    return jnp.stack([lead_len, tail_len], axis=-1).astype(jnp.int32)


def levels(rng, dims, cuts, smallest, high):
    loudness, own = 1.0, jax.random.fold_in(rng, 6)
    for dim, parts in cuts:
        steps = jnp.exp(jax.random.uniform(jax.random.fold_in(own, dim), (parts,), jnp.float32, smallest / len(cuts), high / len(cuts)))
        loudness = loudness * jnp.repeat(steps, dims[dim] // parts).reshape([-1 if axis == dim else 1 for axis in range(len(dims))])
    return loudness


def scatter_about(rng, dims, spread, limit, pieces=(), kind=jnp.bfloat16):
    level = levels(rng, dims, pieces, -0.22, 0.18) if pieces else 1.0
    entries = jax.random.normal(rng, dims, jnp.float32) * spread * level
    return jnp.minimum(jnp.maximum(entries, -limit), limit).astype(kind)


def setup_inputs(seed: int = 0) -> dict:
    keys = jax.random.split(jax.random.key(seed), 7)
    tokens = scatter_about(keys[0], (ROWS, D), 1.0, 6.0, ((0, 1024),))
    cotangent = scatter_about(keys[1], (ROWS, D), 1.0, 6.0, ((0, 1024),))
    w_in = scatter_about(keys[2], (D, 4 * E), D ** -0.5, 0.1875)
    w_out = scatter_about(keys[3], (E, D), E ** -0.5, 0.25)
    lengths = draw_lengths(jax.random.fold_in(keys[6], 71), 0)
    page_place = jax.vmap(lambda own: jax.random.permutation(own, N_BAL))(jax.random.split(keys[5], N_GRP * N_BAL)).reshape((N_GRP, N_BAL, N_BAL)).astype(jnp.int32)
    return {"tokens": tokens, "cotangent": cotangent, "w_in": w_in, "w_out": w_out, "lengths": lengths, "page_place": page_place}


EPS = 1e-05

def layer_norm(values):
    average = lax.optimization_barrier(jnp.mean(values, axis=-1, keepdims=True))
    centered = values - average
    return centered * lax.rsqrt(lax.optimization_barrier(jnp.mean(centered * centered, axis=-1, keepdims=True)) + EPS)

def branch(tokens_in, w_in, allowed, head_count):
    block_count, block_length, model_width = tokens_in.shape
    inner_width = w_in.shape[1] // 4
    head_size = inner_width // head_count
    normed = layer_norm(tokens_in.astype(jnp.float32)).astype(jnp.bfloat16)
    projected = jnp.dot(normed.reshape(block_count * block_length, model_width), w_in, preferred_element_type=jnp.float32)
    projected = jax.nn.silu(projected).astype(jnp.bfloat16)
    projected = projected.reshape(block_count, block_length, 4, head_count, head_size)
    update = projected[:, :, 0].reshape(block_count, block_length, inner_width)
    value_rows = projected[:, :, 1]
    query_rows = projected[:, :, 2]
    key_rows = projected[:, :, 3]
    scores = jnp.einsum('bihd,bjhd->bhij', query_rows.astype(jnp.float32), key_rows.astype(jnp.float32)) * head_size ** (-0.5)
    weights = jnp.where(allowed[:, None], jax.nn.silu(scores), 0.0).astype(jnp.bfloat16)
    mixed_rows = jnp.einsum('bhij,bjhd->bihd', weights.astype(jnp.float32), value_rows.astype(jnp.float32))
    mixed_rows = mixed_rows.reshape(block_count, block_length, inner_width)
    return (layer_norm(mixed_rows) * update.astype(jnp.float32)).astype(jnp.bfloat16)

def reference(tokens, cotangent, w_in, w_out, lengths, page_place):
    peer_count = N_BAL
    page_rows = RB // peer_count
    inner_width = w_out.shape[0]
    row_ids = jnp.arange(RB, dtype=jnp.int32)
    causal = row_ids[None, :] <= row_ids[:, None]
    peer_ids = jnp.arange(peer_count, dtype=jnp.int32)
    tokens_grouped = tokens.reshape(N_GRP, peer_count, peer_count, page_rows, D)
    cot_grouped = cotangent.reshape(N_GRP, peer_count, peer_count, page_rows, D)

    def per_group(running_sum, inputs):
        tok_group, cot_group, length_group, place_group = inputs
        match_table = place_group[:, :, None] == peer_ids[None, None, :]
        source_page = lax.optimization_barrier(jnp.sum(jnp.where(match_table, peer_ids[None, :, None], 0), axis=1)).astype(jnp.int32)

        def pack(grouped):
            by_dest = jnp.swapaxes(grouped, 0, 1)
            picked = jnp.take_along_axis(by_dest, source_page[:, :, None, None], axis=1)
            return picked.reshape(peer_count, RB, grouped.shape[-1])

        def unpack(packed):
            paged_rows = packed.reshape(peer_count, peer_count, page_rows, packed.shape[-1])
            returned = jnp.take_along_axis(paged_rows, place_group[:, :, None, None], axis=1)
            return jnp.swapaxes(returned, 0, 1).reshape(peer_count * peer_count * page_rows, packed.shape[-1])
        later_rows = row_ids[None, :] >= length_group[:, 0:1]
        allowed = causal[None] & (later_rows[:, :, None] == later_rows[:, None, :])
        tok_packed = pack(tok_group)
        cot_packed = pack(cot_group)

        def local_branch(tokens_in):
            return branch(tokens_in, w_in, allowed, HEADS)
        gated, pull_back = jax.vjp(local_branch, tok_packed)
        flat_gated = gated.reshape(-1, inner_width)
        flat_cot = cot_packed.reshape(-1, D)
        out_rows = tok_packed.astype(jnp.float32) + jnp.dot(flat_gated, w_out, preferred_element_type=jnp.float32).reshape(tok_packed.shape)
        out_rows = out_rows.astype(jnp.bfloat16)
        grad_gated = lax.dot_general(flat_cot, w_out, (((1,), (1,)), ((), ())), preferred_element_type=jnp.float32)
        grad_gated = grad_gated.astype(jnp.bfloat16).reshape(gated.shape)
        grad_branch = pull_back(grad_gated)[0]
        grad_rows = (cot_packed.astype(jnp.float32) + grad_branch.astype(jnp.float32)).astype(jnp.bfloat16)
        running_sum = running_sum + lax.dot_general(flat_gated, flat_cot, (((0,), (0,)), ((), ())), preferred_element_type=jnp.float32)
        return (running_sum, (unpack(out_rows), unpack(grad_rows)))
    start_sum = jnp.zeros((inner_width, D), jnp.float32)
    total_grad, (output_all, grad_all) = lax.scan(per_group, start_sum, (tokens_grouped, cot_grouped, lengths, page_place))
    weight_grad = (total_grad * (1.0 / math.sqrt(N_GRP * N_BAL * RB))).astype(jnp.bfloat16)
    return (output_all.reshape(tokens.shape), grad_all.reshape(tokens.shape), weight_grad)
```

```python
import functools
import math

import jax
import jax.numpy as jnp
from jax import lax
from jax.experimental import pallas as pl
from jax.experimental.pallas import tpu as pltpu
from jax.sharding import PartitionSpec as P

HEADS = 4
EPS = 1e-05
MESH = pl.DeviceIdType.MESH
F32 = jnp.float32
BF16 = jnp.bfloat16

NX, NY, NZ, NC = 4, 8, 16, 2
NB = NX * NY
PAGE = 8
ROWS = NB * PAGE
D = 1024
E = 512
HS = E // HEADS
TOK, GG, GATED, GRAD, RA, RX, RY, RZ, GZ, GY, GX, GC = range(12)


def nt(a, b):
    return lax.dot_general(a, b, (((1,), (1,)), ((), ())), preferred_element_type=F32)


def tn(a, b):
    return lax.dot_general(a, b, (((0,), (0,)), ((), ())), preferred_element_type=F32)


def nn(a, b):
    return jnp.dot(a, b, preferred_element_type=F32)


def sigmoid(v):
    return 0.5 * jnp.tanh(0.5 * v) + 0.5


def row_mean(v):
    return jnp.mean(v, axis=-1, keepdims=True)


def kernel(
    scale_out,
    tok3_hbm, tok_hbm, cot_hbm, w_in_hbm, w_out_hbm, len_hbm, place_hbm,
    out_hbm, grad_hbm, wg_hbm,
    cot, tok, w_in, w_out, lens, place,
    tokr, gg_s, ggr, gated_s, gatedr, grad_s, gradr,
    zin, inv1, normed, proj, dsilu, mask, wts, fac, mixed, inv2, dm, dpre, dn,
    gown, p_send, p_own, r_a, a_send, r_x, b_send, r_y, c_send, r_z, gz, wg,
    out_v, grad_v,
    ssem, rsem, lsem,
):
    grp = lax.axis_index("grp")
    me = lax.axis_index("bal")
    z, core = grp // NC, lax.rem(grp, NC)
    x, y = me // NY, lax.rem(me, NY)

    loads = [
        pltpu.make_async_copy(src, dst, lsem.at[i])
        for i, (src, dst) in enumerate(
            (
                (cot_hbm, cot),
                (w_out_hbm, w_out),
                (w_in_hbm, w_in),
                (tok_hbm, tok),
                (len_hbm.at[grp], lens),
                (place_hbm.at[grp], place),
            )
        )
    ]
    for load in loads:
        load.start()

    def bal_peer(k):
        dy = lax.rem(3 * k, NY)
        dx = lax.rem(k + k // NY, NX)
        return lax.rem(x + dx, NX) * NY + lax.rem(y + dy, NY)

    def z_peer(d):
        return lax.rem(z + d, NZ) * NC + core

    barrier = pltpu.get_barrier_semaphore()

    @pl.loop(1, NB)
    def _(k):
        pl.semaphore_signal(barrier, inc=1, device_id={"bal": bal_peer(k)}, device_id_type=MESH)

    @pl.loop(1, NZ)
    def _(d):
        pl.semaphore_signal(barrier, inc=1, device_id={"grp": z_peer(d)}, device_id_type=MESH)

    partner = z * NC + 1 - core
    pl.semaphore_signal(barrier, inc=1, device_id={"grp": partner}, device_id_type=MESH)
    pl.semaphore_wait(barrier, NB - 1 + NZ - 1 + 1)

    def spread(src, dst, i):
        @pl.loop(1, NB)
        def _(k):
            peer = bal_peer(k)
            pltpu.make_async_remote_copy(
                src_ref=src.at[peer], dst_ref=dst.at[me],
                send_sem=ssem.at[i], recv_sem=rsem.at[i],
                device_id={"bal": peer}, device_id_type=MESH,
            ).start()

        pltpu.make_async_copy(src.at[me], dst.at[me], rsem.at[i]).start()

    def remote(src, dst, i, device):
        pltpu.make_async_remote_copy(
            src_ref=src, dst_ref=dst, send_sem=ssem.at[i], recv_sem=rsem.at[i],
            device_id=device, device_id_type=MESH,
        ).start()

    def wait_recv(ref, i):
        pltpu.make_async_copy(ref, ref, rsem.at[i]).wait()

    def wait_send(ref, i):
        pltpu.make_async_copy(ref, ref, ssem.at[i]).wait()

    spread(tok3_hbm, tokr, TOK)

    loads[0].wait()
    loads[1].wait()
    gg_s[...] = nt(cot[...], w_out[...]).reshape(NB, PAGE, E).astype(BF16)
    spread(gg_s, ggr, GG)

    loads[4].wait()
    loads[5].wait()
    lane2 = lax.broadcasted_iota(jnp.int32, (2, NB), 1)
    row2 = lax.broadcasted_iota(jnp.int32, (2, NB), 0)
    first = jnp.sum(
        jnp.where((lane2 == me) & (row2 == 0), lens[...], 0).astype(F32), axis=(0, 1), keepdims=True
    )
    sub = lax.broadcasted_iota(jnp.int32, (NB, NB), 0)
    place_row = jnp.sum(
        jnp.where(sub == me, place[...], 0).astype(F32), axis=0, keepdims=True
    )
    r_id = lax.broadcasted_iota(jnp.int32, (ROWS, NB), 0)
    p_id = lax.broadcasted_iota(jnp.int32, (ROWS, NB), 1)
    picked = jnp.where((r_id // PAGE) == p_id, jnp.broadcast_to(place_row, (ROWS, NB)), 0.0)
    page_col = jnp.sum(picked, axis=1, keepdims=True)
    in_page = lax.rem(lax.broadcasted_iota(jnp.int32, (ROWS, 1), 0), PAGE).astype(F32)
    pos_col = page_col * PAGE + in_page
    e_p = lax.broadcasted_iota(jnp.int32, (NB, ROWS), 0)
    e_r = lax.broadcasted_iota(jnp.int32, (NB, ROWS), 1)
    spread_pages = jnp.where((e_r // PAGE) == e_p, 1.0, 0.0).astype(BF16)
    page_row = nn(jnp.broadcast_to(place_row, (PAGE, NB)).astype(BF16), spread_pages)[0:1]
    in_page_row = lax.rem(lax.broadcasted_iota(jnp.int32, (1, ROWS), 1), PAGE).astype(F32)
    pos_row = page_row * PAGE + in_page_row
    start_col = jnp.where(pos_col >= first, jnp.broadcast_to(first, (ROWS, 1)), 0.0)
    mask[...] = jnp.where((pos_row <= pos_col) & (pos_row >= start_col), 1.0, 0.0)

    loads[2].wait()
    wait_recv(tokr, TOK)

    @pl.loop(0, ROWS // 32)
    def _(i):
        rows = pl.ds(pl.multiple_of(i * 32, 32), 32)
        v = tokr[pl.ds(i * 4, 4)].astype(F32).reshape(32, D)
        c = v - row_mean(v)
        inv = lax.rsqrt(row_mean(c * c) + EPS)
        n = c * inv
        zin[rows, :] = n
        inv1[rows, :] = jnp.broadcast_to(inv, (32, 128))
        normed[rows, :] = n.astype(BF16)

    @pl.loop(0, 4 * E // 256)
    def _(j):
        cols = pl.ds(pl.multiple_of(j * 256, 256), 256)
        pre = nn(normed[...], w_in[:, cols])
        sig = sigmoid(pre)
        proj[:, cols] = (pre * sig).astype(BF16)
        dsilu[:, cols] = sig * (1.0 + pre * (1.0 - sig))

    def head_cols(block, h):
        return pl.ds(pl.multiple_of(block * E + h * HS, HS), HS)

    @pl.loop(0, HEADS)
    def _(h):
        s = nt(proj[:, head_cols(2, h)], proj[:, head_cols(3, h)]) * (HS ** -0.5)
        sig = sigmoid(s)
        allowed = mask[...]
        w = (s * sig * allowed).astype(BF16)
        wts[h] = w
        fac[h] = allowed * (HS ** -0.5) * sig * (1.0 + s * (1.0 - sig))
        mixed[:, head_cols(0, h)] = nn(w, proj[:, head_cols(1, h)])

    @pl.loop(0, ROWS // 32)
    def _(i):
        rows = pl.ds(pl.multiple_of(i * 32, 32), 32)
        v = mixed[rows, :]
        c = v - row_mean(v)
        inv = lax.rsqrt(row_mean(c * c) + EPS)
        n = c * inv
        mixed[rows, :] = n
        inv2[rows, :] = jnp.broadcast_to(inv, (32, 128))
        g = n * proj[rows, 0:E].astype(F32)
        gated_s[pl.ds(i * 4, 4)] = g.reshape(4, PAGE, E).astype(BF16)

    spread(gated_s, gatedr, GATED)

    wait_recv(ggr, GG)

    @pl.loop(0, ROWS // 32)
    def _(i):
        rows = pl.ds(pl.multiple_of(i * 32, 32), 32)
        g = ggr[pl.ds(i * 4, 4)].astype(F32).reshape(32, E)
        n = mixed[rows, :]
        du = (g * n).astype(BF16).astype(F32)
        dpre[rows, 0:E] = (du * dsilu[rows, 0:E]).astype(BF16)
        dz = g * proj[rows, 0:E].astype(F32)
        back = inv2[rows, 0:1] * (dz - row_mean(dz) - n * row_mean(dz * n))
        dm[rows, :] = back.astype(BF16)

    @pl.loop(0, HEADS)
    def _(h):
        dmh = dm[:, head_cols(0, h)]
        vc, qc, kc = head_cols(1, h), head_cols(2, h), head_cols(3, h)
        dv = tn(wts[h], dmh).astype(BF16).astype(F32)
        dpre[:, vc] = (dv * dsilu[:, vc]).astype(BF16)
        dw = nt(dmh, proj[:, vc]).astype(BF16).astype(F32)
        ds = (dw * fac[h]).astype(BF16)
        dq = nn(ds, proj[:, kc]).astype(BF16).astype(F32)
        dpre[:, qc] = (dq * dsilu[:, qc]).astype(BF16)
        dk = tn(ds, proj[:, qc]).astype(BF16).astype(F32)
        dpre[:, kc] = (dk * dsilu[:, kc]).astype(BF16)

    @pl.loop(0, D // 256)
    def _(j):
        cols = pl.ds(pl.multiple_of(j * 256, 256), 256)
        dn[:, cols] = nt(dpre[...], w_in[cols, :]).astype(BF16)

    @pl.loop(0, ROWS // 32)
    def _(i):
        rows = pl.ds(pl.multiple_of(i * 32, 32), 32)
        d = dn[rows, :].astype(F32)
        n = zin[rows, :]
        back = inv1[rows, 0:1] * (d - row_mean(d) - n * row_mean(d * n))
        grad_s[pl.ds(i * 4, 4)] = back.reshape(4, PAGE, D).astype(BF16)

    spread(grad_s, gradr, GRAD)

    wait_recv(gatedr, GATED)

    @pl.loop(0, ROWS // 32)
    def _(i):
        rows = pl.ds(pl.multiple_of(i * 32, 32), 32)
        gown[rows, :] = gatedr[pl.ds(i * 4, 4)].astype(F32).reshape(32, E).astype(BF16)

    half = E // NC
    nh = half // PAGE
    other_cols = pl.ds(pl.multiple_of((1 - core) * half, half), half)
    own_cols = pl.ds(pl.multiple_of(core * half, half), half)
    p_send[...] = tn(gown[:, other_cols], cot[...]).reshape(nh, PAGE, D).astype(BF16)
    remote(p_send, r_a, RA, {"grp": partner})
    p_own[...] = tn(gown[:, own_cols], cot[...]).reshape(nh, PAGE, D)

    loads[3].wait()

    @pl.loop(0, D // 256)
    def _(j):
        cols = pl.ds(pl.multiple_of(j * 256, 256), 256)
        out_v[:, cols] = (tok[:, cols].astype(F32) + nn(gown[...], w_out[:, cols])).astype(BF16)

    out_copy = pltpu.make_async_copy(out_v, out_hbm, lsem.at[0])
    out_copy.start()

    wait_recv(r_a, RA)

    @pl.loop(0, nh // 4)
    def _(i):
        blocks = pl.ds(i * 4, 4)
        a = p_own[blocks] + r_a[blocks].astype(F32)
        p_own[blocks] = a
        a_send[blocks] = a.astype(BF16)

    for d in range(1, NX):
        px = lax.rem(x + d, NX)
        remote(
            a_send.at[pl.ds(px * NY, NY)], r_x.at[pl.ds((d - 1) * NY, NY)], RX, {"bal": px * NY + y}
        )
    wait_recv(r_x, RX)

    @pl.loop(0, NY)
    def _(i):
        b = p_own[x * NY + i]
        for d in range(NX - 1):
            b = b + r_x[d * NY + i].astype(F32)
        p_own[x * NY + i] = b
        b_send[i] = b.astype(BF16)

    for d in range(1, NY):
        py = lax.rem(y + d, NY)
        remote(b_send.at[py], r_y.at[d - 1], RY, {"bal": x * NY + py})
    wait_recv(r_y, RY)
    total = p_own[me]
    for d in range(NY - 1):
        total = total + r_y[d].astype(F32)
    for p in range(8):
        c_send[p] = total[:, p * 128 : (p + 1) * 128]
    zp = lax.rem(z, 8)
    r_z[z] = c_send[zp]

    @pl.loop(1, NZ)
    def _(d):
        pz = lax.rem(z + d, NZ)
        remote(c_send.at[lax.rem(pz, 8)], r_z.at[z], RZ, {"grp": pz * NC + core})

    wait_recv(r_z.at[pl.ds(0, NZ - 1)], RZ)
    piece = r_z[0]
    for p in range(1, NZ):
        piece = piece + r_z[p]
    gz[zp] = (piece * scale_out).astype(BF16)

    for d in (1, -1, 2, -2, 3, -3, 4):
        remote(gz.at[zp], gz.at[zp], GZ, {"grp": z_peer(d + NZ)})
    wait_recv(gz.at[pl.ds(0, 7)], GZ)
    block = core * nh + me
    for p in range(8):
        wg[block, :, p * 128 : (p + 1) * 128] = gz[p]
    for d in range(1, NY):
        py = lax.rem(y + d, NY)
        remote(wg.at[block], wg.at[block], GY, {"bal": x * NY + py})
    wait_recv(wg.at[pl.ds(0, NY - 1)], GY)
    xs = pl.ds(core * nh + x * NY, NY)
    for d in range(1, NX):
        px = lax.rem(x + d, NX)
        remote(wg.at[xs], wg.at[xs], GX, {"bal": px * NY + y})
    wait_recv(wg.at[pl.ds(0, (NX - 1) * NY)], GX)
    cs = pl.ds(core * nh, nh)
    remote(wg.at[cs], wg.at[cs], GC, {"grp": partner})

    wait_recv(gradr, GRAD)

    @pl.loop(0, ROWS // 32)
    def _(i):
        rows = pl.ds(pl.multiple_of(i * 32, 32), 32)
        b = gradr[pl.ds(i * 4, 4)].astype(F32).reshape(32, D)
        grad_v[rows, :] = (cot[rows, :].astype(F32) + b).astype(BF16)

    grad_copy = pltpu.make_async_copy(grad_v, grad_hbm, lsem.at[1])
    grad_copy.start()
    wait_recv(wg.at[pl.ds(0, nh)], GC)
    wg_copy = pltpu.make_async_copy(wg, wg_hbm, lsem.at[2])
    wg_copy.start()

    for ref, i in ((tok3_hbm, TOK), (gg_s, GG), (gated_s, GATED), (grad_s, GRAD)):
        wait_send(ref.at[pl.ds(0, NB - 1)], i)
    wait_send(p_send, RA)
    wait_send(a_send.at[pl.ds(0, (NX - 1) * NY)], RX)
    wait_send(b_send.at[pl.ds(0, NY - 1)], RY)
    wait_send(r_z.at[pl.ds(0, NZ - 1)], RZ)
    wait_send(gz.at[pl.ds(0, 7)], GZ)
    wait_send(wg.at[pl.ds(0, NY - 1)], GY)
    wait_send(wg.at[pl.ds(0, (NX - 1) * NY)], GX)
    wait_send(wg.at[pl.ds(0, nh)], GC)
    out_copy.wait()
    grad_copy.wait()
    wg_copy.wait()


def body(tokens, cotangent, w_in, w_out, lengths, page_place):
    nblk = E // PAGE
    nh = nblk // NC
    scale_out = 1.0 / math.sqrt(NZ * NC * NB * ROWS)
    vm = pltpu.VMEM
    scratch = [
        vm((ROWS, D), BF16), vm((ROWS, D), BF16), vm((D, 4 * E), BF16), vm((E, D), BF16),
        vm((2, NB), jnp.int32), vm((NB, NB), jnp.int32),
        vm((NB, PAGE, D), BF16),
        vm((NB, PAGE, E), BF16), vm((NB, PAGE, E), BF16),
        vm((NB, PAGE, E), BF16), vm((NB, PAGE, E), BF16),
        vm((NB, PAGE, D), BF16), vm((NB, PAGE, D), BF16),
        vm((ROWS, D), F32), vm((ROWS, 128), F32), vm((ROWS, D), BF16),
        vm((ROWS, 4 * E), BF16), vm((ROWS, 4 * E), F32), vm((ROWS, ROWS), F32),
        vm((HEADS, ROWS, ROWS), BF16), vm((HEADS, ROWS, ROWS), F32),
        vm((ROWS, E), F32), vm((ROWS, 128), F32), vm((ROWS, E), BF16),
        vm((ROWS, 4 * E), BF16), vm((ROWS, D), BF16),
        vm((ROWS, E), BF16),
        vm((nh, PAGE, D), BF16), vm((nh, PAGE, D), F32), vm((nh, PAGE, D), BF16),
        vm((nh, PAGE, D), BF16), vm(((NX - 1) * NY, PAGE, D), BF16),
        vm((NY, PAGE, D), BF16), vm((NY - 1, PAGE, D), BF16),
        vm((8, PAGE, 128), F32), vm((NZ, PAGE, 128), F32), vm((8, PAGE, 128), BF16),
        vm((nblk, PAGE, D), BF16),
        vm((ROWS, D), BF16), vm((ROWS, D), BF16),
        pltpu.SemaphoreType.DMA((12,)), pltpu.SemaphoreType.DMA((12,)), pltpu.SemaphoreType.DMA((6,)),
    ]
    hbm = pl.BlockSpec(memory_space=pltpu.HBM)
    output, grad_tokens, weight_grad = pl.pallas_call(
        functools.partial(kernel, scale_out),
        out_shape=(
            jax.ShapeDtypeStruct((ROWS, D), BF16),
            jax.ShapeDtypeStruct((ROWS, D), BF16),
            jax.ShapeDtypeStruct((nblk, PAGE, D), BF16),
        ),
        in_specs=[hbm] * 7,
        out_specs=(hbm, hbm, hbm),
        scratch_shapes=scratch,
        compiler_params=pltpu.CompilerParams(
            collective_id=0, has_side_effects=True, vmem_limit_bytes=60 * 1024 * 1024
        ),
    )(
        tokens.reshape(NB, PAGE, D), tokens, cotangent, w_in, w_out,
        jnp.swapaxes(lengths, 1, 2), page_place,
    )
    return output, grad_tokens, weight_grad.reshape(E, D)


def solution(mesh):
    placed = (P(("grp", "bal"), None), P(("grp", "bal"), None), P(), P(), P(), P())
    return jax.shard_map(
        body,
        mesh=mesh,
        in_specs=placed,
        out_specs=(P(("grp", "bal"), None), P(("grp", "bal"), None), P()),
        check_vma=False,
    )
```

```python
import functools
import math

import jax
import jax.numpy as jnp
from jax import lax
from jax.experimental import pallas as pl
from jax.experimental.pallas import tpu as pltpu
from jax.sharding import PartitionSpec as P

HEADS = 4
EPS = 1e-05
MESH = pl.DeviceIdType.MESH
F32 = jnp.float32
BF16 = jnp.bfloat16

NX, NY, NZ, NC = 4, 8, 16, 2
NB = NX * NY
ZL = 4
ZH = max(NZ // ZL, 1)
PAGE = 8
ROWS = NB * PAGE
D = 1024
E = 512
HS = E // HEADS
TOK, GG, GATED, GRAD = range(4)
HALVES = 2
RA, RX, RY, RZ, RV, GZ, GY, GX, GC = range(4, 4 + 9 * HALVES, HALVES)
HD = D // HALVES
NP = HD // 128


def nt(a, b):
    return lax.dot_general(a, b, (((1,), (1,)), ((), ())), preferred_element_type=F32)


def tn(a, b):
    return lax.dot_general(a, b, (((0,), (0,)), ((), ())), preferred_element_type=F32)


def nn(a, b):
    return jnp.dot(a, b, preferred_element_type=F32)


def sigmoid(v):
    return 0.5 * jnp.tanh(0.5 * v) + 0.5


def row_mean(v):
    return jnp.mean(v, axis=-1, keepdims=True)


def kernel(
    scale_out,
    tok3_hbm, tok_hbm, cot_hbm, w_in_hbm, w_out_hbm, len_hbm, place_hbm,
    out_hbm, grad_hbm, wg_hbm,
    cot, tok, w_in, w_out, lens, place,
    tokr, gg_s, ggr, gated_s, gatedr, grad_s, gradr,
    zin, inv1, normed, proj, dsilu, mask, wts, fac, mixed, inv2, dm, dpre, dn,
    gown, p_send, p_own, r_a, a_send, r_x, b_send, r_y, c_send, r_z, r_v, gz, wg,
    out_v, grad_v,
    ssem, rsem, lsem,
):
    grp = lax.axis_index("grp")
    me = lax.axis_index("bal")
    z, core = grp // NC, lax.rem(grp, NC)
    x, y = me // NY, lax.rem(me, NY)
    zh, zl = z // ZL, lax.rem(z, ZL)

    loads = [
        pltpu.make_async_copy(src, dst, lsem.at[i])
        for i, (src, dst) in enumerate(
            (
                (cot_hbm, cot),
                (w_out_hbm, w_out),
                (w_in_hbm, w_in),
                (tok_hbm, tok),
                (len_hbm.at[grp], lens),
                (place_hbm.at[grp], place),
            )
        )
    ]
    for load in loads:
        load.start()

    def bal_peer(k):
        dy = lax.rem(3 * k, NY)
        dx = lax.rem(k + k // NY, NX)
        return lax.rem(x + dx, NX) * NY + lax.rem(y + dy, NY)

    def run_peer(d):
        return (zh * ZL + lax.rem(zl + d, ZL)) * NC + core

    def cross_peer(d):
        return (lax.rem(zh + d, ZH) * ZL + zl) * NC + core

    barrier = pltpu.get_barrier_semaphore()

    @pl.loop(1, NB)
    def _(k):
        pl.semaphore_signal(barrier, inc=1, device_id={"bal": bal_peer(k)}, device_id_type=MESH)

    z_peers = [run_peer(d) for d in range(1, ZL)] + [cross_peer(d) for d in range(1, ZH)] if NZ > 1 else []
    for peer in z_peers:
        pl.semaphore_signal(barrier, inc=1, device_id={"grp": peer}, device_id_type=MESH)
    partner = z * NC + 1 - core
    pl.semaphore_signal(barrier, inc=1, device_id={"grp": partner}, device_id_type=MESH)
    pl.semaphore_wait(barrier, NB - 1 + len(z_peers) + 1)

    def spread(src, dst, i, low=1, high=NB):
        @pl.loop(low, high)
        def _(k):
            peer = bal_peer(k)
            pltpu.make_async_remote_copy(
                src_ref=src.at[peer], dst_ref=dst.at[me],
                send_sem=ssem.at[i], recv_sem=rsem.at[i],
                device_id={"bal": peer}, device_id_type=MESH,
            ).start()

        if high == NB:
            pltpu.make_async_copy(src.at[me], dst.at[me], rsem.at[i]).start()

    def remote(src, dst, i, device):
        pltpu.make_async_remote_copy(
            src_ref=src, dst_ref=dst, send_sem=ssem.at[i], recv_sem=rsem.at[i],
            device_id=device, device_id_type=MESH,
        ).start()

    def wait_recv(ref, i):
        pltpu.make_async_copy(ref, ref, rsem.at[i]).wait()

    def wait_send(ref, i):
        pltpu.make_async_copy(ref, ref, ssem.at[i]).wait()

    spread(tok3_hbm, tokr, TOK)

    loads[0].wait()
    loads[1].wait()
    gg_s[...] = nt(cot[...], w_out[...]).reshape(NB, PAGE, E).astype(BF16)
    spread(gg_s, ggr, GG)

    loads[4].wait()
    loads[5].wait()
    lane2 = lax.broadcasted_iota(jnp.int32, (2, NB), 1)
    row2 = lax.broadcasted_iota(jnp.int32, (2, NB), 0)
    first = jnp.sum(
        jnp.where((lane2 == me) & (row2 == 0), lens[...], 0).astype(F32), axis=(0, 1), keepdims=True
    )
    sub = lax.broadcasted_iota(jnp.int32, (NB, NB), 0)
    place_row = jnp.sum(
        jnp.where(sub == me, place[...], 0).astype(F32), axis=0, keepdims=True
    )
    r_id = lax.broadcasted_iota(jnp.int32, (ROWS, NB), 0)
    p_id = lax.broadcasted_iota(jnp.int32, (ROWS, NB), 1)
    picked = jnp.where((r_id // PAGE) == p_id, jnp.broadcast_to(place_row, (ROWS, NB)), 0.0)
    page_col = jnp.sum(picked, axis=1, keepdims=True)
    in_page = lax.rem(lax.broadcasted_iota(jnp.int32, (ROWS, 1), 0), PAGE).astype(F32)
    pos_col = page_col * PAGE + in_page
    e_p = lax.broadcasted_iota(jnp.int32, (NB, ROWS), 0)
    e_r = lax.broadcasted_iota(jnp.int32, (NB, ROWS), 1)
    spread_pages = jnp.where((e_r // PAGE) == e_p, 1.0, 0.0).astype(BF16)
    page_row = nn(jnp.broadcast_to(place_row, (PAGE, NB)).astype(BF16), spread_pages)[0:1]
    in_page_row = lax.rem(lax.broadcasted_iota(jnp.int32, (1, ROWS), 1), PAGE).astype(F32)
    pos_row = page_row * PAGE + in_page_row
    start_col = jnp.where(pos_col >= first, jnp.broadcast_to(first, (ROWS, 1)), 0.0)
    mask[...] = jnp.where((pos_row <= pos_col) & (pos_row >= start_col), 1.0, 0.0)

    loads[2].wait()
    wait_recv(tokr, TOK)

    for i in range(ROWS // 32):
        rows = pl.ds(i * 32, 32)
        v = tokr[pl.ds(i * 4, 4)].astype(F32).reshape(32, D)
        c = v - row_mean(v)
        inv = lax.rsqrt(row_mean(c * c) + EPS)
        n = c * inv
        zin[rows, :] = n
        inv1[rows, :] = jnp.broadcast_to(inv, (32, 128))
        normed[rows, :] = n.astype(BF16)

    for j in range(4 * E // 256):
        cols = pl.ds(j * 256, 256)
        pre = nn(normed[...], w_in[:, cols])
        sig = sigmoid(pre)
        proj[:, cols] = (pre * sig).astype(BF16)
        dsilu[:, cols] = sig * (1.0 + pre * (1.0 - sig))

    def head_cols(block, h):
        return pl.ds(block * E + h * HS, HS)

    for h in range(HEADS):
        s = nt(proj[:, head_cols(2, h)], proj[:, head_cols(3, h)]) * (HS ** -0.5)
        sig = sigmoid(s)
        allowed = mask[...]
        w = (s * sig * allowed).astype(BF16)
        wts[h] = w
        fac[h] = allowed * (HS ** -0.5) * sig * (1.0 + s * (1.0 - sig))
        mixed[:, head_cols(0, h)] = nn(w, proj[:, head_cols(1, h)])

    for i in range(ROWS // 32):
        rows = pl.ds(i * 32, 32)
        v = mixed[rows, :]
        c = v - row_mean(v)
        inv = lax.rsqrt(row_mean(c * c) + EPS)
        n = c * inv
        mixed[rows, :] = n
        inv2[rows, :] = jnp.broadcast_to(inv, (32, 128))
        g = n * proj[rows, 0:E].astype(F32)
        gated_s[pl.ds(i * 4, 4)] = g.reshape(4, PAGE, E).astype(BF16)

    spread(gated_s, gatedr, GATED)

    wait_recv(ggr, GG)

    for i in range(ROWS // 32):
        rows = pl.ds(i * 32, 32)
        g = ggr[pl.ds(i * 4, 4)].astype(F32).reshape(32, E)
        n = mixed[rows, :]
        du = (g * n).astype(BF16).astype(F32)
        dpre[rows, 0:E] = (du * dsilu[rows, 0:E]).astype(BF16)
        dz = g * proj[rows, 0:E].astype(F32)
        back = inv2[rows, 0:1] * (dz - row_mean(dz) - n * row_mean(dz * n))
        dm[rows, :] = back.astype(BF16)

    for h in range(HEADS):
        dmh = dm[:, head_cols(0, h)]
        vc, qc, kc = head_cols(1, h), head_cols(2, h), head_cols(3, h)
        dv = tn(wts[h], dmh).astype(BF16).astype(F32)
        dpre[:, vc] = (dv * dsilu[:, vc]).astype(BF16)
        dw = nt(dmh, proj[:, vc]).astype(BF16).astype(F32)
        ds = (dw * fac[h]).astype(BF16)
        dq = nn(ds, proj[:, kc]).astype(BF16).astype(F32)
        dpre[:, qc] = (dq * dsilu[:, qc]).astype(BF16)
        dk = tn(ds, proj[:, qc]).astype(BF16).astype(F32)
        dpre[:, kc] = (dk * dsilu[:, kc]).astype(BF16)

    for j in range(D // 256):
        cols = pl.ds(j * 256, 256)
        dn[:, cols] = nt(dpre[...], w_in[cols, :]).astype(BF16)

    for i in range(ROWS // 32):
        rows = pl.ds(i * 32, 32)
        d = dn[rows, :].astype(F32)
        n = zin[rows, :]
        back = inv1[rows, 0:1] * (d - row_mean(d) - n * row_mean(d * n))
        grad_s[pl.ds(i * 4, 4)] = back.reshape(4, PAGE, D).astype(BF16)

    spread(grad_s, gradr, GRAD)

    wait_recv(gatedr, GATED)

    for i in range(ROWS // 32):
        rows = pl.ds(i * 32, 32)
        gown[rows, :] = gatedr[pl.ds(i * 4, 4)].astype(F32).reshape(32, E).astype(BF16)

    half = E // NC
    nh = half // PAGE
    other_cols = pl.ds(pl.multiple_of((1 - core) * half, half), half)
    own_cols = pl.ds(pl.multiple_of(core * half, half), half)

    def term(cols, h):
        return tn(gown[:, cols], cot[:, h * HD : (h + 1) * HD]).reshape(nh, PAGE, HD)

    for h in range(HALVES):
        p_send[h] = term(other_cols, h).astype(BF16)
        remote(p_send.at[h], r_a.at[h], RA + h, {"grp": partner})
    for h in range(HALVES):
        p_own[h] = term(own_cols, h)

    for h in range(HALVES):
        wait_recv(r_a.at[h], RA + h)
        for i in range(0, nh, 4):
            a = p_own[h, i : i + 4] + r_a[h, i : i + 4].astype(F32)
            p_own[h, i : i + 4] = a
            a_send[h, i : i + 4] = a.astype(BF16)
        for d in (1, 3, 2):
            px = lax.rem(x + d, NX)
            remote(
                a_send.at[h, pl.ds(px * NY, NY)], r_x.at[h, pl.ds((d - 1) * NY, NY)],
                RX + h, {"bal": px * NY + y},
            )

    loads[3].wait()
    for j in range(D // 256):
        cols = pl.ds(j * 256, 256)
        out_v[:, cols] = (tok[:, cols].astype(F32) + nn(gown[...], w_out[:, cols])).astype(BF16)
    out_copy = pltpu.make_async_copy(out_v, out_hbm, lsem.at[0])
    out_copy.start()

    for h in range(HALVES):
        wait_recv(r_x.at[h], RX + h)
        b = p_own[h, pl.ds(x * NY, NY)]
        for d in range(NX - 1):
            b = b + r_x[h, d * NY : (d + 1) * NY].astype(F32)
        p_own[h, pl.ds(x * NY, NY)] = b
        b_send[h] = b.astype(BF16)
        for d in range(1, NY):
            py = lax.rem(y + d, NY)
            remote(b_send.at[h, py], r_y.at[h, d - 1], RY + h, {"bal": x * NY + py})

    for h in range(HALVES):
        wait_recv(r_y.at[h], RY + h)
        total = p_own[h, me]
        for d in range(NY - 1):
            total = total + r_y[h, d].astype(F32)
        for p in range(NP):
            c_send[h, p] = total[:, p * 128 : (p + 1) * 128]
        r_z[h, zl] = c_send[h, zl]
        if NZ > 1:
            for d in range(1, ZL):
                remote(c_send.at[h, lax.rem(zl + d, ZL)], r_z.at[h, zl], RZ + h, {"grp": run_peer(d)})

    for h in range(HALVES):
        piece = r_z[h, 0] if NZ == 1 else None
        if NZ > 1:
            wait_recv(r_z.at[h, pl.ds(0, ZL - 1)], RZ + h)
            piece = r_z[h, 0] + r_z[h, 1] + r_z[h, 2] + r_z[h, 3]
        r_v[h, zh] = piece
        for d in range(1, ZH):
            remote(r_v.at[h, zh], r_v.at[h, zh], RV + h, {"grp": cross_peer(d)})

    for h in range(HALVES):
        if NZ > 1:
            wait_recv(r_v.at[h, pl.ds(0, ZH - 1)], RV + h)
        piece = r_v[h, 0]
        for p in range(1, ZH):
            piece = piece + r_v[h, p]
        gz[h, zl] = (piece * scale_out).astype(BF16)
        if NZ > 1:
            for d in range(1, ZL):
                remote(gz.at[h, zl], gz.at[h, zl], GZ + h, {"grp": run_peer(d)})

    block = core * nh + me
    for h in range(HALVES):
        if NZ > 1:
            wait_recv(gz.at[h, pl.ds(0, ZL - 1)], GZ + h)
        for p in range(NP):
            wg[h, block, :, p * 128 : (p + 1) * 128] = gz[h, p]
        for d in range(1, NY):
            py = lax.rem(y + d, NY)
            remote(wg.at[h, block], wg.at[h, block], GY + h, {"bal": x * NY + py})

    xs = pl.ds(core * nh + x * NY, NY)
    for h in range(HALVES):
        wait_recv(wg.at[h, pl.ds(0, NY - 1)], GY + h)
        for d in (1, 3, 2):
            px = lax.rem(x + d, NX)
            remote(wg.at[h, xs], wg.at[h, xs], GX + h, {"bal": px * NY + y})

    cs = pl.ds(core * nh, nh)
    for h in range(HALVES):
        wait_recv(wg.at[h, pl.ds(0, (NX - 1) * NY)], GX + h)
        remote(wg.at[h, cs], wg.at[h, cs], GC + h, {"grp": partner})

    wait_recv(gradr, GRAD)
    for i in range(ROWS // 32):
        rows = pl.ds(i * 32, 32)
        b = gradr[pl.ds(i * 4, 4)].astype(F32).reshape(32, D)
        grad_v[rows, :] = (cot[rows, :].astype(F32) + b).astype(BF16)
    grad_copy = pltpu.make_async_copy(grad_v, grad_hbm, lsem.at[1])
    grad_copy.start()

    wg_copies = []
    for h in range(HALVES):
        wait_recv(wg.at[h, pl.ds(0, nh)], GC + h)
        wg_copies.append(
            pltpu.make_async_copy(wg.at[h], wg_hbm.at[:, :, pl.ds(h * HD, HD)], lsem.at[2 + h])
        )
        wg_copies[h].start()

    for ref, i in ((tok3_hbm, TOK), (gg_s, GG), (gated_s, GATED), (grad_s, GRAD)):
        wait_send(ref.at[pl.ds(0, NB - 1)], i)
    for h in range(HALVES):
        wait_send(p_send.at[h], RA + h)
        wait_send(r_x.at[h], RX + h)
        wait_send(r_y.at[h], RY + h)
        if NZ > 1:
            wait_send(r_z.at[h, pl.ds(0, ZL - 1)], RZ + h)
            wait_send(r_v.at[h, pl.ds(0, ZH - 1)], RV + h)
            wait_send(gz.at[h, pl.ds(0, ZL - 1)], GZ + h)
        wait_send(wg.at[h, pl.ds(0, NY - 1)], GY + h)
        wait_send(wg.at[h, pl.ds(0, (NX - 1) * NY)], GX + h)
        wait_send(wg.at[h, pl.ds(0, nh)], GC + h)
    for copy in (out_copy, grad_copy, *wg_copies):
        copy.wait()


def copy_kernel(n, *refs):
    sources, targets, held, sems = refs[:n], refs[n : 2 * n], refs[2 * n : 3 * n], refs[3 * n]
    parts = []
    for i in range(n):
        step = sources[i].shape[0] // 2
        for j in range(2):
            part = pl.ds(j * step, step)
            loads, stores = sems.at[0, 2 * i + j], sems.at[1, 2 * i + j]
            parts.append(
                (
                    pltpu.make_async_copy(sources[i].at[part], held[i].at[part], loads),
                    pltpu.make_async_copy(held[i].at[part], targets[i].at[part], stores),
                )
            )
    for load, _ in parts:
        load.start()
    for load, store in parts:
        load.wait()
        store.start()
    for _, store in parts:
        store.wait()


def body(tokens, cotangent, w_in, w_out, lengths, page_place):
    nblk = E // PAGE
    nh = nblk // NC
    scale_out = 1.0 / math.sqrt(NZ * NC * NB * ROWS)
    vm = pltpu.VMEM
    scratch = [
        vm((ROWS, D), BF16), vm((ROWS, D), BF16), vm((D, 4 * E), BF16), vm((E, D), BF16),
        vm((2, NB), jnp.int32), vm((NB, NB), jnp.int32),
        vm((NB, PAGE, D), BF16),
        vm((NB, PAGE, E), BF16), vm((NB, PAGE, E), BF16),
        vm((NB, PAGE, E), BF16), vm((NB, PAGE, E), BF16),
        vm((NB, PAGE, D), BF16), vm((NB, PAGE, D), BF16),
        vm((ROWS, D), F32), vm((ROWS, 128), F32), vm((ROWS, D), BF16),
        vm((ROWS, 4 * E), BF16), vm((ROWS, 4 * E), F32), vm((ROWS, ROWS), F32),
        vm((HEADS, ROWS, ROWS), BF16), vm((HEADS, ROWS, ROWS), F32),
        vm((ROWS, E), F32), vm((ROWS, 128), F32), vm((ROWS, E), BF16),
        vm((ROWS, 4 * E), BF16), vm((ROWS, D), BF16),
        vm((ROWS, E), BF16),
        vm((HALVES, nh, PAGE, HD), BF16), vm((HALVES, nh, PAGE, HD), F32),
        vm((HALVES, nh, PAGE, HD), BF16), vm((HALVES, nh, PAGE, HD), BF16),
        vm((HALVES, (NX - 1) * NY, PAGE, HD), BF16),
        vm((HALVES, NY, PAGE, HD), BF16), vm((HALVES, NY - 1, PAGE, HD), BF16),
        vm((HALVES, NP, PAGE, 128), F32), vm((HALVES, ZL, PAGE, 128), F32),
        vm((HALVES, ZH, PAGE, 128), F32),
        vm((HALVES, NP, PAGE, 128), BF16),
        vm((HALVES, nblk, PAGE, HD), BF16),
        vm((ROWS, D), BF16), vm((ROWS, D), BF16),
        pltpu.SemaphoreType.DMA((4 + 9 * HALVES,)), pltpu.SemaphoreType.DMA((4 + 9 * HALVES,)),
        pltpu.SemaphoreType.DMA((8,)),
    ]
    hbm = pl.BlockSpec(memory_space=pltpu.HBM)
    results = pl.pallas_call(
        functools.partial(kernel, scale_out),
        out_shape=(
            jax.ShapeDtypeStruct((ROWS, D), BF16),
            jax.ShapeDtypeStruct((ROWS, D), BF16),
            jax.ShapeDtypeStruct((nblk, PAGE, D), BF16),
        ),
        in_specs=[hbm] * 7,
        out_specs=(hbm, hbm, hbm),
        scratch_shapes=scratch,
        compiler_params=pltpu.CompilerParams(
            collective_id=0, has_side_effects=True, vmem_limit_bytes=60 * 1024 * 1024
        ),
    )(
        tokens.reshape(NB, PAGE, D), tokens, cotangent, w_in, w_out,
        jnp.swapaxes(lengths, 1, 2), page_place,
    )
    output, grad_tokens, weight_grad = pl.pallas_call(
        functools.partial(copy_kernel, len(results)),
        out_shape=tuple(jax.ShapeDtypeStruct(r.shape, r.dtype) for r in results),
        in_specs=[hbm] * len(results),
        out_specs=(hbm,) * len(results),
        scratch_shapes=[pltpu.VMEM(r.shape, r.dtype) for r in results]
        + [pltpu.SemaphoreType.DMA((2, 2 * len(results)))],
        compiler_params=pltpu.CompilerParams(vmem_limit_bytes=60 * 1024 * 1024),
    )(*results)
    return output, grad_tokens, weight_grad.reshape(E, D)


def solution(mesh):
    placed = (P(("grp", "bal"), None), P(("grp", "bal"), None), P(), P(), P(), P())
    return jax.shard_map(
        body,
        mesh=mesh,
        in_specs=placed,
        out_specs=(P(("grp", "bal"), None), P(("grp", "bal"), None), P()),
        check_vma=False,
    )
```

```python
import functools
import math

import jax
import jax.numpy as jnp
from jax import lax
from jax.experimental import pallas as pl
from jax.experimental.pallas import tpu as pltpu
from jax.sharding import PartitionSpec as P

HEADS = 4
EPS = 1e-05
MESH = pl.DeviceIdType.MESH
F32 = jnp.float32
BF16 = jnp.bfloat16

NX, NY, NZ, NC = 4, 8, 16, 2
NB = NX * NY
ZL = 4
ZH = max(NZ // ZL, 1)
PAGE = 8
ROWS = NB * PAGE
D = 1024
E = 512
HS = E // HEADS
TOK, GG, GATED, GRAD = range(4)
HALVES = 2
RA, RX, RY, RZ, RV, GZ, GY, GX, GC = range(4, 4 + 9 * HALVES, HALVES)
HD = D // HALVES
NP = HD // 128


def nt(a, b):
    return lax.dot_general(a, b, (((1,), (1,)), ((), ())), preferred_element_type=F32)


def tn(a, b):
    return lax.dot_general(a, b, (((0,), (0,)), ((), ())), preferred_element_type=F32)


def nn(a, b):
    return jnp.dot(a, b, preferred_element_type=F32)


def sigmoid(v):
    return 0.5 * jnp.tanh(0.5 * v) + 0.5


def row_mean(v):
    return jnp.mean(v, axis=-1, keepdims=True)


def kernel(
    scale_out,
    tok3_hbm, tok_hbm, cot_hbm, w_in_hbm, w_out_hbm, len_hbm, place_hbm,
    out_hbm, grad_hbm, wg_hbm,
    cot, tok, w_in, w_out, lens, place,
    tokr, gg_s, ggr, gated_s, gatedr, grad_s, gradr,
    zin, inv1, normed, proj, dsilu, mask, wts, fac, mixed, inv2, dm, dpre, dn,
    gown, p_send, p_own, r_a, a_send, r_x, b_send, r_y, c_send, r_z, r_v, gz, wg,
    out_v, grad_v,
    ssem, rsem, lsem,
):
    grp = lax.axis_index("grp")
    me = lax.axis_index("bal")
    z, core = grp // NC, lax.rem(grp, NC)
    x, y = me // NY, lax.rem(me, NY)
    zh, zl = z // ZL, lax.rem(z, ZL)

    loads = [
        pltpu.make_async_copy(src, dst, lsem.at[i])
        for i, (src, dst) in enumerate(
            (
                (cot_hbm, cot),
                (w_out_hbm, w_out),
                (w_in_hbm, w_in),
                (tok_hbm, tok),
                (len_hbm.at[grp], lens),
                (place_hbm.at[grp], place),
            )
        )
    ]
    for load in loads:
        load.start()

    def bal_peer(k):
        dy = lax.rem(3 * k, NY)
        dx = lax.rem(k + k // NY, NX)
        return lax.rem(x + dx, NX) * NY + lax.rem(y + dy, NY)

    def run_peer(d):
        return (zh * ZL + lax.rem(zl + d, ZL)) * NC + core

    def cross_peer(d):
        return (lax.rem(zh + d, ZH) * ZL + zl) * NC + core

    barrier = pltpu.get_barrier_semaphore()

    @pl.loop(1, NB)
    def _(k):
        pl.semaphore_signal(barrier, inc=1, device_id={"bal": bal_peer(k)}, device_id_type=MESH)

    z_peers = [run_peer(d) for d in range(1, ZL)] + [cross_peer(d) for d in range(1, ZH)] if NZ > 1 else []
    for peer in z_peers:
        pl.semaphore_signal(barrier, inc=1, device_id={"grp": peer}, device_id_type=MESH)
    partner = z * NC + 1 - core
    pl.semaphore_signal(barrier, inc=1, device_id={"grp": partner}, device_id_type=MESH)
    pl.semaphore_wait(barrier, NB - 1 + len(z_peers) + 1)

    def spread(src, dst, i, low=1, high=NB):
        @pl.loop(low, high)
        def _(k):
            peer = bal_peer(k)
            pltpu.make_async_remote_copy(
                src_ref=src.at[peer], dst_ref=dst.at[me],
                send_sem=ssem.at[i], recv_sem=rsem.at[i],
                device_id={"bal": peer}, device_id_type=MESH,
            ).start()

        if high == NB:
            pltpu.make_async_copy(src.at[me], dst.at[me], rsem.at[i]).start()

    def remote(src, dst, i, device):
        pltpu.make_async_remote_copy(
            src_ref=src, dst_ref=dst, send_sem=ssem.at[i], recv_sem=rsem.at[i],
            device_id=device, device_id_type=MESH,
        ).start()

    def wait_recv(ref, i):
        pltpu.make_async_copy(ref, ref, rsem.at[i]).wait()

    def wait_send(ref, i):
        pltpu.make_async_copy(ref, ref, ssem.at[i]).wait()

    spread(tok3_hbm, tokr, TOK)

    loads[0].wait()
    loads[1].wait()
    gg_s[...] = nt(cot[...], w_out[...]).reshape(NB, PAGE, E).astype(BF16)
    spread(gg_s, ggr, GG)

    loads[4].wait()
    loads[5].wait()
    lane2 = lax.broadcasted_iota(jnp.int32, (2, NB), 1)
    row2 = lax.broadcasted_iota(jnp.int32, (2, NB), 0)
    first = jnp.sum(
        jnp.where((lane2 == me) & (row2 == 0), lens[...], 0).astype(F32), axis=(0, 1), keepdims=True
    )
    sub = lax.broadcasted_iota(jnp.int32, (NB, NB), 0)
    place_row = jnp.sum(
        jnp.where(sub == me, place[...], 0).astype(F32), axis=0, keepdims=True
    )
    r_id = lax.broadcasted_iota(jnp.int32, (ROWS, NB), 0)
    p_id = lax.broadcasted_iota(jnp.int32, (ROWS, NB), 1)
    picked = jnp.where((r_id // PAGE) == p_id, jnp.broadcast_to(place_row, (ROWS, NB)), 0.0)
    page_col = jnp.sum(picked, axis=1, keepdims=True)
    in_page = lax.rem(lax.broadcasted_iota(jnp.int32, (ROWS, 1), 0), PAGE).astype(F32)
    pos_col = page_col * PAGE + in_page
    e_p = lax.broadcasted_iota(jnp.int32, (NB, ROWS), 0)
    e_r = lax.broadcasted_iota(jnp.int32, (NB, ROWS), 1)
    spread_pages = jnp.where((e_r // PAGE) == e_p, 1.0, 0.0).astype(BF16)
    page_row = nn(jnp.broadcast_to(place_row, (PAGE, NB)).astype(BF16), spread_pages)[0:1]
    in_page_row = lax.rem(lax.broadcasted_iota(jnp.int32, (1, ROWS), 1), PAGE).astype(F32)
    pos_row = page_row * PAGE + in_page_row
    start_col = jnp.where(pos_col >= first, jnp.broadcast_to(first, (ROWS, 1)), 0.0)
    mask[...] = jnp.where((pos_row <= pos_col) & (pos_row >= start_col), 1.0, 0.0)

    loads[2].wait()
    wait_recv(tokr, TOK)

    for i in range(ROWS // 32):
        rows = pl.ds(i * 32, 32)
        v = tokr[pl.ds(i * 4, 4)].astype(F32).reshape(32, D)
        c = v - row_mean(v)
        inv = lax.rsqrt(row_mean(c * c) + EPS)
        n = c * inv
        zin[rows, :] = n
        inv1[rows, :] = jnp.broadcast_to(inv, (32, 128))
        normed[rows, :] = n.astype(BF16)

    for j in range(4 * E // 256):
        cols = pl.ds(j * 256, 256)
        pre = nn(normed[...], w_in[:, cols])
        sig = sigmoid(pre)
        proj[:, cols] = (pre * sig).astype(BF16)
        dsilu[:, cols] = sig * (1.0 + pre * (1.0 - sig))

    def head_cols(block, h):
        return pl.ds(block * E + h * HS, HS)

    for h in range(HEADS):
        s = nt(proj[:, head_cols(2, h)], proj[:, head_cols(3, h)]) * (HS ** -0.5)
        sig = sigmoid(s)
        allowed = mask[...]
        w = (s * sig * allowed).astype(BF16)
        wts[h] = w
        fac[h] = allowed * (HS ** -0.5) * sig * (1.0 + s * (1.0 - sig))
        mixed[:, head_cols(0, h)] = nn(w, proj[:, head_cols(1, h)])

    for i in range(ROWS // 32):
        rows = pl.ds(i * 32, 32)
        v = mixed[rows, :]
        c = v - row_mean(v)
        inv = lax.rsqrt(row_mean(c * c) + EPS)
        n = c * inv
        mixed[rows, :] = n
        inv2[rows, :] = jnp.broadcast_to(inv, (32, 128))
        g = n * proj[rows, 0:E].astype(F32)
        gated_s[pl.ds(i * 4, 4)] = g.reshape(4, PAGE, E).astype(BF16)

    spread(gated_s, gatedr, GATED)

    wait_recv(ggr, GG)

    for i in range(ROWS // 32):
        rows = pl.ds(i * 32, 32)
        g = ggr[pl.ds(i * 4, 4)].astype(F32).reshape(32, E)
        n = mixed[rows, :]
        du = (g * n).astype(BF16).astype(F32)
        dpre[rows, 0:E] = (du * dsilu[rows, 0:E]).astype(BF16)
        dz = g * proj[rows, 0:E].astype(F32)
        back = inv2[rows, 0:1] * (dz - row_mean(dz) - n * row_mean(dz * n))
        dm[rows, :] = back.astype(BF16)

    for h in range(HEADS):
        dmh = dm[:, head_cols(0, h)]
        vc, qc, kc = head_cols(1, h), head_cols(2, h), head_cols(3, h)
        dv = tn(wts[h], dmh).astype(BF16).astype(F32)
        dpre[:, vc] = (dv * dsilu[:, vc]).astype(BF16)
        dw = nt(dmh, proj[:, vc]).astype(BF16).astype(F32)
        ds = (dw * fac[h]).astype(BF16)
        dq = nn(ds, proj[:, kc]).astype(BF16).astype(F32)
        dpre[:, qc] = (dq * dsilu[:, qc]).astype(BF16)
        dk = tn(ds, proj[:, qc]).astype(BF16).astype(F32)
        dpre[:, kc] = (dk * dsilu[:, kc]).astype(BF16)

    for j in range(D // 256):
        cols = pl.ds(j * 256, 256)
        dn[:, cols] = nt(dpre[...], w_in[cols, :]).astype(BF16)

    for i in range(ROWS // 32):
        rows = pl.ds(i * 32, 32)
        d = dn[rows, :].astype(F32)
        n = zin[rows, :]
        back = inv1[rows, 0:1] * (d - row_mean(d) - n * row_mean(d * n))
        grad_s[pl.ds(i * 4, 4)] = back.reshape(4, PAGE, D).astype(BF16)

    wait_recv(gatedr, GATED)

    for i in range(ROWS // 32):
        rows = pl.ds(i * 32, 32)
        gown[rows, :] = gatedr[pl.ds(i * 4, 4)].astype(F32).reshape(32, E).astype(BF16)

    half = E // NC
    nh = half // PAGE
    other_cols = pl.ds(pl.multiple_of((1 - core) * half, half), half)
    own_cols = pl.ds(pl.multiple_of(core * half, half), half)

    def term(cols, h):
        return tn(gown[:, cols], cot[:, h * HD : (h + 1) * HD]).reshape(nh, PAGE, HD)

    for h in range(HALVES):
        p_send[h] = term(other_cols, h).astype(BF16)
        remote(p_send.at[h], r_a.at[h], RA + h, {"grp": partner})
    for h in range(HALVES):
        p_own[h] = term(own_cols, h)

    for h in range(HALVES):
        wait_recv(r_a.at[h], RA + h)
        for i in range(0, nh, 4):
            a = p_own[h, i : i + 4] + r_a[h, i : i + 4].astype(F32)
            p_own[h, i : i + 4] = a
            a_send[h, i : i + 4] = a.astype(BF16)
        for d in (2, 1, 3):
            px = lax.rem(x + d, NX)
            remote(
                a_send.at[h, pl.ds(px * NY, NY)], r_x.at[h, pl.ds((d - 1) * NY, NY)],
                RX + h, {"bal": px * NY + y},
            )

    loads[3].wait()
    for j in range(D // 256):
        cols = pl.ds(j * 256, 256)
        out_v[:, cols] = (tok[:, cols].astype(F32) + nn(gown[...], w_out[:, cols])).astype(BF16)
    out_copy = pltpu.make_async_copy(out_v, out_hbm, lsem.at[0])
    out_copy.start()

    for h in range(HALVES):
        wait_recv(r_x.at[h], RX + h)
        b = p_own[h, pl.ds(x * NY, NY)]
        for d in range(NX - 1):
            b = b + r_x[h, d * NY : (d + 1) * NY].astype(F32)
        p_own[h, pl.ds(x * NY, NY)] = b
        b_send[h] = b.astype(BF16)
        for d in (4, 3, 5, 2, 6, 1, 7):
            py = lax.rem(y + d, NY)
            remote(b_send.at[h, py], r_y.at[h, d - 1], RY + h, {"bal": x * NY + py})

    spread(grad_s, gradr, GRAD)

    for h in range(HALVES):
        wait_recv(r_y.at[h], RY + h)
        total = p_own[h, me]
        for d in range(NY - 1):
            total = total + r_y[h, d].astype(F32)
        for p in range(NP):
            c_send[h, p] = total[:, p * 128 : (p + 1) * 128]
        r_z[h, zl] = c_send[h, zl]
        if NZ > 1:
            for d in range(1, ZL):
                remote(c_send.at[h, lax.rem(zl + d, ZL)], r_z.at[h, zl], RZ + h, {"grp": run_peer(d)})

    for h in range(HALVES):
        piece = r_z[h, 0] if NZ == 1 else None
        if NZ > 1:
            wait_recv(r_z.at[h, pl.ds(0, ZL - 1)], RZ + h)
            piece = r_z[h, 0] + r_z[h, 1] + r_z[h, 2] + r_z[h, 3]
        r_v[h, zh] = piece
        for d in sorted(range(1, ZH), key=lambda d: -min(d, ZH - d)):
            remote(r_v.at[h, zh], r_v.at[h, zh], RV + h, {"grp": cross_peer(d)})

    for h in range(HALVES):
        if NZ > 1:
            wait_recv(r_v.at[h, pl.ds(0, ZH - 1)], RV + h)
        piece = r_v[h, 0]
        for p in range(1, ZH):
            piece = piece + r_v[h, p]
        gz[h, zl] = (piece * scale_out).astype(BF16)
        if NZ > 1:
            for d in range(1, ZL):
                remote(gz.at[h, zl], gz.at[h, zl], GZ + h, {"grp": run_peer(d)})

    block = core * nh + me
    for h in range(HALVES):
        if NZ > 1:
            wait_recv(gz.at[h, pl.ds(0, ZL - 1)], GZ + h)
        for p in range(NP):
            wg[h, block, :, p * 128 : (p + 1) * 128] = gz[h, p]
        for d in (4, 3, 5, 2, 6, 1, 7):
            py = lax.rem(y + d, NY)
            remote(wg.at[h, block], wg.at[h, block], GY + h, {"bal": x * NY + py})

    xs = pl.ds(core * nh + x * NY, NY)
    for h in range(HALVES):
        wait_recv(wg.at[h, pl.ds(0, NY - 1)], GY + h)
        for d in (2, 1, 3):
            px = lax.rem(x + d, NX)
            remote(wg.at[h, xs], wg.at[h, xs], GX + h, {"bal": px * NY + y})

    cs = pl.ds(core * nh, nh)
    for h in range(HALVES):
        wait_recv(wg.at[h, pl.ds(0, (NX - 1) * NY)], GX + h)
        remote(wg.at[h, cs], wg.at[h, cs], GC + h, {"grp": partner})

    wait_recv(gradr, GRAD)
    for i in range(ROWS // 32):
        rows = pl.ds(i * 32, 32)
        b = gradr[pl.ds(i * 4, 4)].astype(F32).reshape(32, D)
        grad_v[rows, :] = (cot[rows, :].astype(F32) + b).astype(BF16)
    grad_copy = pltpu.make_async_copy(grad_v, grad_hbm, lsem.at[1])
    grad_copy.start()

    wg_copies = []
    for h in range(HALVES):
        wait_recv(wg.at[h, pl.ds(0, nh)], GC + h)
        wg_copies.append(
            pltpu.make_async_copy(wg.at[h], wg_hbm.at[:, :, pl.ds(h * HD, HD)], lsem.at[2 + h])
        )
        wg_copies[h].start()

    for ref, i in ((tok3_hbm, TOK), (gg_s, GG), (gated_s, GATED), (grad_s, GRAD)):
        wait_send(ref.at[pl.ds(0, NB - 1)], i)
    for h in range(HALVES):
        wait_send(p_send.at[h], RA + h)
        wait_send(r_x.at[h], RX + h)
        wait_send(r_y.at[h], RY + h)
        if NZ > 1:
            wait_send(r_z.at[h, pl.ds(0, ZL - 1)], RZ + h)
            wait_send(r_v.at[h, pl.ds(0, ZH - 1)], RV + h)
            wait_send(gz.at[h, pl.ds(0, ZL - 1)], GZ + h)
        wait_send(wg.at[h, pl.ds(0, NY - 1)], GY + h)
        wait_send(wg.at[h, pl.ds(0, (NX - 1) * NY)], GX + h)
        wait_send(wg.at[h, pl.ds(0, nh)], GC + h)
    for copy in (out_copy, grad_copy, *wg_copies):
        copy.wait()


def copy_kernel(n, *refs):
    sources, targets, held, sems = refs[:n], refs[n : 2 * n], refs[2 * n : 3 * n], refs[3 * n]
    parts = []
    for i in range(n):
        step = sources[i].shape[0] // 2
        for j in range(2):
            part = pl.ds(j * step, step)
            loads, stores = sems.at[0, 2 * i + j], sems.at[1, 2 * i + j]
            parts.append(
                (
                    pltpu.make_async_copy(sources[i].at[part], held[i].at[part], loads),
                    pltpu.make_async_copy(held[i].at[part], targets[i].at[part], stores),
                )
            )
    for load, _ in parts:
        load.start()
    for load, store in parts:
        load.wait()
        store.start()
    for _, store in parts:
        store.wait()


def body(tokens, cotangent, w_in, w_out, lengths, page_place):
    nblk = E // PAGE
    nh = nblk // NC
    scale_out = 1.0 / math.sqrt(NZ * NC * NB * ROWS)
    vm = pltpu.VMEM
    scratch = [
        vm((ROWS, D), BF16), vm((ROWS, D), BF16), vm((D, 4 * E), BF16), vm((E, D), BF16),
        vm((2, NB), jnp.int32), vm((NB, NB), jnp.int32),
        vm((NB, PAGE, D), BF16),
        vm((NB, PAGE, E), BF16), vm((NB, PAGE, E), BF16),
        vm((NB, PAGE, E), BF16), vm((NB, PAGE, E), BF16),
        vm((NB, PAGE, D), BF16), vm((NB, PAGE, D), BF16),
        vm((ROWS, D), F32), vm((ROWS, 128), F32), vm((ROWS, D), BF16),
        vm((ROWS, 4 * E), BF16), vm((ROWS, 4 * E), F32), vm((ROWS, ROWS), F32),
        vm((HEADS, ROWS, ROWS), BF16), vm((HEADS, ROWS, ROWS), F32),
        vm((ROWS, E), F32), vm((ROWS, 128), F32), vm((ROWS, E), BF16),
        vm((ROWS, 4 * E), BF16), vm((ROWS, D), BF16),
        vm((ROWS, E), BF16),
        vm((HALVES, nh, PAGE, HD), BF16), vm((HALVES, nh, PAGE, HD), F32),
        vm((HALVES, nh, PAGE, HD), BF16), vm((HALVES, nh, PAGE, HD), BF16),
        vm((HALVES, (NX - 1) * NY, PAGE, HD), BF16),
        vm((HALVES, NY, PAGE, HD), BF16), vm((HALVES, NY - 1, PAGE, HD), BF16),
        vm((HALVES, NP, PAGE, 128), F32), vm((HALVES, ZL, PAGE, 128), F32),
        vm((HALVES, ZH, PAGE, 128), F32),
        vm((HALVES, NP, PAGE, 128), BF16),
        vm((HALVES, nblk, PAGE, HD), BF16),
        vm((ROWS, D), BF16), vm((ROWS, D), BF16),
        pltpu.SemaphoreType.DMA((4 + 9 * HALVES,)), pltpu.SemaphoreType.DMA((4 + 9 * HALVES,)),
        pltpu.SemaphoreType.DMA((8,)),
    ]
    hbm = pl.BlockSpec(memory_space=pltpu.HBM)
    results = pl.pallas_call(
        functools.partial(kernel, scale_out),
        out_shape=(
            jax.ShapeDtypeStruct((ROWS, D), BF16),
            jax.ShapeDtypeStruct((ROWS, D), BF16),
            jax.ShapeDtypeStruct((nblk, PAGE, D), BF16),
        ),
        in_specs=[hbm] * 7,
        out_specs=(hbm, hbm, hbm),
        scratch_shapes=scratch,
        compiler_params=pltpu.CompilerParams(
            collective_id=0, has_side_effects=True, vmem_limit_bytes=60 * 1024 * 1024
        ),
    )(
        tokens.reshape(NB, PAGE, D), tokens, cotangent, w_in, w_out,
        jnp.swapaxes(lengths, 1, 2), page_place,
    )
    output, grad_tokens, weight_grad = pl.pallas_call(
        functools.partial(copy_kernel, len(results)),
        out_shape=tuple(jax.ShapeDtypeStruct(r.shape, r.dtype) for r in results),
        in_specs=[hbm] * len(results),
        out_specs=(hbm,) * len(results),
        scratch_shapes=[pltpu.VMEM(r.shape, r.dtype) for r in results]
        + [pltpu.SemaphoreType.DMA((2, 2 * len(results)))],
        compiler_params=pltpu.CompilerParams(vmem_limit_bytes=60 * 1024 * 1024),
    )(*results)
    return output, grad_tokens, weight_grad.reshape(E, D)


def solution(mesh):
    placed = (P(("grp", "bal"), None), P(("grp", "bal"), None), P(), P(), P(), P())
    return jax.shard_map(
        body,
        mesh=mesh,
        in_specs=placed,
        out_specs=(P(("grp", "bal"), None), P(("grp", "bal"), None), P()),
        check_vma=False,
    )
```

```python
import functools
import math

import jax
import jax.numpy as jnp
from jax import lax
from jax.experimental import pallas as pl
from jax.experimental.pallas import tpu as pltpu
from jax.sharding import PartitionSpec as P

HEADS = 4
EPS = 1e-05
MESH = pl.DeviceIdType.MESH
F32 = jnp.float32
BF16 = jnp.bfloat16

NX, NY, NZ, NC = 4, 8, 16, 2
NB = NX * NY
ZL = 4
ZH = max(NZ // ZL, 1)
PAGE = 8
ROWS = NB * PAGE
D = 1024
E = 512
HS = E // HEADS
TOK, GG, GATED, GRAD = range(4)
HALVES = 2
RA, RX, RY, RZ, RV, GZ, GY, GX, GC = range(4, 4 + 9 * HALVES, HALVES)
HD = D // HALVES
NP = HD // 128


def nt(a, b):
    return lax.dot_general(a, b, (((1,), (1,)), ((), ())), preferred_element_type=F32)


def tn(a, b):
    return lax.dot_general(a, b, (((0,), (0,)), ((), ())), preferred_element_type=F32)


def nn(a, b):
    return jnp.dot(a, b, preferred_element_type=F32)


def sigmoid(v):
    return 0.5 * jnp.tanh(0.5 * v) + 0.5


def row_mean(v):
    return jnp.mean(v, axis=-1, keepdims=True)


def kernel(
    scale_out,
    tok3_hbm, tok_hbm, cot_hbm, w_in_hbm, w_out_hbm, len_hbm, place_hbm,
    out_hbm, grad_hbm, wg_hbm,
    cot, tok, w_in, w_out, lens, place,
    tokr, gg_s, ggr, gated_s, gatedr, grad_s, gradr,
    zin, inv1, normed, proj, dsilu, mask, wts, fac, mixed, inv2, dm, dpre, dn,
    gown, p_send, p_own, r_a, a_send, r_x, b_send, r_y, c_send, r_z, r_v, gz, wg,
    out_v, grad_v,
    ssem, rsem, lsem,
):
    grp = lax.axis_index("grp")
    me = lax.axis_index("bal")
    z, core = grp // NC, lax.rem(grp, NC)
    x, y = me // NY, lax.rem(me, NY)
    zh, zl = z // ZL, lax.rem(z, ZL)

    loads = [
        pltpu.make_async_copy(src, dst, lsem.at[i])
        for i, (src, dst) in enumerate(
            (
                (cot_hbm, cot),
                (w_out_hbm, w_out),
                (w_in_hbm, w_in),
                (tok_hbm, tok),
                (len_hbm.at[grp], lens),
                (place_hbm.at[grp], place),
            )
        )
    ]
    for load in loads:
        load.start()

    def bal_peer(k):
        dy = lax.rem(3 * k, NY)
        dx = lax.rem(k + k // NY, NX)
        return lax.rem(x + dx, NX) * NY + lax.rem(y + dy, NY)

    def run_peer(d):
        return (zh * ZL + lax.rem(zl + d, ZL)) * NC + core

    def cross_peer(d):
        return (lax.rem(zh + d, ZH) * ZL + zl) * NC + core

    barrier = pltpu.get_barrier_semaphore()

    @pl.loop(1, NB)
    def _(k):
        pl.semaphore_signal(barrier, inc=1, device_id={"bal": bal_peer(k)}, device_id_type=MESH)

    z_peers = [run_peer(d) for d in range(1, ZL)] + [cross_peer(d) for d in range(1, ZH)] if NZ > 1 else []
    for peer in z_peers:
        pl.semaphore_signal(barrier, inc=1, device_id={"grp": peer}, device_id_type=MESH)
    partner = z * NC + 1 - core
    pl.semaphore_signal(barrier, inc=1, device_id={"grp": partner}, device_id_type=MESH)
    pl.semaphore_wait(barrier, NB - 1 + len(z_peers) + 1)

    def spread(src, dst, i, low=1, high=NB):
        @pl.loop(low, high)
        def _(k):
            peer = bal_peer(k)
            pltpu.make_async_remote_copy(
                src_ref=src.at[peer], dst_ref=dst.at[me],
                send_sem=ssem.at[i], recv_sem=rsem.at[i],
                device_id={"bal": peer}, device_id_type=MESH,
            ).start()

        if high == NB:
            pltpu.make_async_copy(src.at[me], dst.at[me], rsem.at[i]).start()

    def remote(src, dst, i, device):
        pltpu.make_async_remote_copy(
            src_ref=src, dst_ref=dst, send_sem=ssem.at[i], recv_sem=rsem.at[i],
            device_id=device, device_id_type=MESH,
        ).start()

    def wait_recv(ref, i):
        pltpu.make_async_copy(ref, ref, rsem.at[i]).wait()

    def wait_send(ref, i):
        pltpu.make_async_copy(ref, ref, ssem.at[i]).wait()

    spread(tok3_hbm, tokr, TOK)

    loads[0].wait()
    loads[1].wait()
    gg_s[...] = nt(cot[...], w_out[...]).reshape(NB, PAGE, E).astype(BF16)
    spread(gg_s, ggr, GG)

    loads[4].wait()
    loads[5].wait()
    lane2 = lax.broadcasted_iota(jnp.int32, (2, NB), 1)
    row2 = lax.broadcasted_iota(jnp.int32, (2, NB), 0)
    first = jnp.sum(
        jnp.where((lane2 == me) & (row2 == 0), lens[...], 0).astype(F32), axis=(0, 1), keepdims=True
    )
    sub = lax.broadcasted_iota(jnp.int32, (NB, NB), 0)
    place_row = jnp.sum(
        jnp.where(sub == me, place[...], 0).astype(F32), axis=0, keepdims=True
    )
    r_id = lax.broadcasted_iota(jnp.int32, (ROWS, NB), 0)
    p_id = lax.broadcasted_iota(jnp.int32, (ROWS, NB), 1)
    picked = jnp.where((r_id // PAGE) == p_id, jnp.broadcast_to(place_row, (ROWS, NB)), 0.0)
    page_col = jnp.sum(picked, axis=1, keepdims=True)
    in_page = lax.rem(lax.broadcasted_iota(jnp.int32, (ROWS, 1), 0), PAGE).astype(F32)
    pos_col = page_col * PAGE + in_page
    e_p = lax.broadcasted_iota(jnp.int32, (NB, ROWS), 0)
    e_r = lax.broadcasted_iota(jnp.int32, (NB, ROWS), 1)
    spread_pages = jnp.where((e_r // PAGE) == e_p, 1.0, 0.0).astype(BF16)
    page_row = nn(jnp.broadcast_to(place_row, (PAGE, NB)).astype(BF16), spread_pages)[0:1]
    in_page_row = lax.rem(lax.broadcasted_iota(jnp.int32, (1, ROWS), 1), PAGE).astype(F32)
    pos_row = page_row * PAGE + in_page_row
    start_col = jnp.where(pos_col >= first, jnp.broadcast_to(first, (ROWS, 1)), 0.0)
    mask[...] = jnp.where((pos_row <= pos_col) & (pos_row >= start_col), 1.0, 0.0)

    loads[2].wait()
    wait_recv(tokr, TOK)

    for i in range(ROWS // 32):
        rows = pl.ds(i * 32, 32)
        v = tokr[pl.ds(i * 4, 4)].astype(F32).reshape(32, D)
        c = v - row_mean(v)
        inv = lax.rsqrt(row_mean(c * c) + EPS)
        n = c * inv
        zin[rows, :] = n
        inv1[rows, :] = jnp.broadcast_to(inv, (32, 128))
        normed[rows, :] = n.astype(BF16)

    for j in range(4 * E // 256):
        cols = pl.ds(j * 256, 256)
        pre = nn(normed[...], w_in[:, cols])
        sig = sigmoid(pre)
        proj[:, cols] = (pre * sig).astype(BF16)
        dsilu[:, cols] = sig * (1.0 + pre * (1.0 - sig))

    def head_cols(block, h):
        return pl.ds(block * E + h * HS, HS)

    for h in range(HEADS):
        s = nt(proj[:, head_cols(2, h)], proj[:, head_cols(3, h)]) * (HS ** -0.5)
        sig = sigmoid(s)
        allowed = mask[...]
        w = (s * sig * allowed).astype(BF16)
        wts[h] = w
        fac[h] = allowed * (HS ** -0.5) * sig * (1.0 + s * (1.0 - sig))
        mixed[:, head_cols(0, h)] = nn(w, proj[:, head_cols(1, h)])

    for i in range(ROWS // 32):
        rows = pl.ds(i * 32, 32)
        v = mixed[rows, :]
        c = v - row_mean(v)
        inv = lax.rsqrt(row_mean(c * c) + EPS)
        n = c * inv
        mixed[rows, :] = n
        inv2[rows, :] = jnp.broadcast_to(inv, (32, 128))
        g = n * proj[rows, 0:E].astype(F32)
        gated_s[pl.ds(i * 4, 4)] = g.reshape(4, PAGE, E).astype(BF16)

    spread(gated_s, gatedr, GATED)

    wait_recv(gatedr, GATED)

    for i in range(ROWS // 32):
        rows = pl.ds(i * 32, 32)
        gown[rows, :] = gatedr[pl.ds(i * 4, 4)].astype(F32).reshape(32, E).astype(BF16)

    half = E // NC
    nh = half // PAGE
    other_cols = pl.ds(pl.multiple_of((1 - core) * half, half), half)
    own_cols = pl.ds(pl.multiple_of(core * half, half), half)

    def term(cols, h):
        return tn(gown[:, cols], cot[:, h * HD : (h + 1) * HD]).reshape(nh, PAGE, HD)

    for h in range(HALVES):
        p_send[h] = term(other_cols, h).astype(BF16)
        remote(p_send.at[h], r_a.at[h], RA + h, {"grp": partner})
    for h in range(HALVES):
        p_own[h] = term(own_cols, h)

    for h in range(HALVES):
        wait_recv(r_a.at[h], RA + h)
        for i in range(0, nh, 4):
            a = p_own[h, i : i + 4] + r_a[h, i : i + 4].astype(F32)
            p_own[h, i : i + 4] = a
            a_send[h, i : i + 4] = a.astype(BF16)
        for d in (2, 1, 3):
            px = lax.rem(x + d, NX)
            remote(
                a_send.at[h, pl.ds(px * NY, NY)], r_x.at[h, pl.ds((d - 1) * NY, NY)],
                RX + h, {"bal": px * NY + y},
            )

    wait_recv(ggr, GG)

    for i in range(ROWS // 32):
        rows = pl.ds(i * 32, 32)
        g = ggr[pl.ds(i * 4, 4)].astype(F32).reshape(32, E)
        n = mixed[rows, :]
        du = (g * n).astype(BF16).astype(F32)
        dpre[rows, 0:E] = (du * dsilu[rows, 0:E]).astype(BF16)
        dz = g * proj[rows, 0:E].astype(F32)
        back = inv2[rows, 0:1] * (dz - row_mean(dz) - n * row_mean(dz * n))
        dm[rows, :] = back.astype(BF16)

    for h in range(HEADS):
        dmh = dm[:, head_cols(0, h)]
        vc, qc, kc = head_cols(1, h), head_cols(2, h), head_cols(3, h)
        dv = tn(wts[h], dmh).astype(BF16).astype(F32)
        dpre[:, vc] = (dv * dsilu[:, vc]).astype(BF16)
        dw = nt(dmh, proj[:, vc]).astype(BF16).astype(F32)
        ds = (dw * fac[h]).astype(BF16)
        dq = nn(ds, proj[:, kc]).astype(BF16).astype(F32)
        dpre[:, qc] = (dq * dsilu[:, qc]).astype(BF16)
        dk = tn(ds, proj[:, qc]).astype(BF16).astype(F32)
        dpre[:, kc] = (dk * dsilu[:, kc]).astype(BF16)

    for j in range(D // 256):
        cols = pl.ds(j * 256, 256)
        dn[:, cols] = nt(dpre[...], w_in[cols, :]).astype(BF16)

    for i in range(ROWS // 32):
        rows = pl.ds(i * 32, 32)
        d = dn[rows, :].astype(F32)
        n = zin[rows, :]
        back = inv1[rows, 0:1] * (d - row_mean(d) - n * row_mean(d * n))
        grad_s[pl.ds(i * 4, 4)] = back.reshape(4, PAGE, D).astype(BF16)

    loads[3].wait()
    for j in range(D // 256):
        cols = pl.ds(j * 256, 256)
        out_v[:, cols] = (tok[:, cols].astype(F32) + nn(gown[...], w_out[:, cols])).astype(BF16)
    out_copy = pltpu.make_async_copy(out_v, out_hbm, lsem.at[0])
    out_copy.start()

    for h in range(HALVES):
        wait_recv(r_x.at[h], RX + h)
        b = p_own[h, pl.ds(x * NY, NY)]
        for d in range(NX - 1):
            b = b + r_x[h, d * NY : (d + 1) * NY].astype(F32)
        p_own[h, pl.ds(x * NY, NY)] = b
        b_send[h] = b.astype(BF16)
        for d in (4, 3, 5, 2, 6, 1, 7):
            py = lax.rem(y + d, NY)
            remote(b_send.at[h, py], r_y.at[h, d - 1], RY + h, {"bal": x * NY + py})

    spread(grad_s, gradr, GRAD)

    for h in range(HALVES):
        wait_recv(r_y.at[h], RY + h)
        total = p_own[h, me]
        for d in range(NY - 1):
            total = total + r_y[h, d].astype(F32)
        for p in range(NP):
            c_send[h, p] = total[:, p * 128 : (p + 1) * 128]
        r_z[h, zl] = c_send[h, zl]
        if NZ > 1:
            for d in range(1, ZL):
                remote(c_send.at[h, lax.rem(zl + d, ZL)], r_z.at[h, zl], RZ + h, {"grp": run_peer(d)})

    for h in range(HALVES):
        piece = r_z[h, 0] if NZ == 1 else None
        if NZ > 1:
            wait_recv(r_z.at[h, pl.ds(0, ZL - 1)], RZ + h)
            piece = r_z[h, 0] + r_z[h, 1] + r_z[h, 2] + r_z[h, 3]
        r_v[h, zh] = piece
        for d in sorted(range(1, ZH), key=lambda d: -min(d, ZH - d)):
            remote(r_v.at[h, zh], r_v.at[h, zh], RV + h, {"grp": cross_peer(d)})

    for h in range(HALVES):
        if NZ > 1:
            wait_recv(r_v.at[h, pl.ds(0, ZH - 1)], RV + h)
        piece = r_v[h, 0]
        for p in range(1, ZH):
            piece = piece + r_v[h, p]
        gz[h, zl] = (piece * scale_out).astype(BF16)
        if NZ > 1:
            for d in range(1, ZL):
                remote(gz.at[h, zl], gz.at[h, zl], GZ + h, {"grp": run_peer(d)})

    block = core * nh + me
    for h in range(HALVES):
        if NZ > 1:
            wait_recv(gz.at[h, pl.ds(0, ZL - 1)], GZ + h)
        for p in range(NP):
            wg[h, block, :, p * 128 : (p + 1) * 128] = gz[h, p]
        for d in (4, 3, 5, 2, 6, 1, 7):
            py = lax.rem(y + d, NY)
            remote(wg.at[h, block], wg.at[h, block], GY + h, {"bal": x * NY + py})

    xs = pl.ds(core * nh + x * NY, NY)
    for h in range(HALVES):
        wait_recv(wg.at[h, pl.ds(0, NY - 1)], GY + h)
        for d in (2, 1, 3):
            px = lax.rem(x + d, NX)
            remote(wg.at[h, xs], wg.at[h, xs], GX + h, {"bal": px * NY + y})

    cs = pl.ds(core * nh, nh)
    for h in range(HALVES):
        wait_recv(wg.at[h, pl.ds(0, (NX - 1) * NY)], GX + h)
        remote(wg.at[h, cs], wg.at[h, cs], GC + h, {"grp": partner})

    wait_recv(gradr, GRAD)
    for i in range(ROWS // 32):
        rows = pl.ds(i * 32, 32)
        b = gradr[pl.ds(i * 4, 4)].astype(F32).reshape(32, D)
        grad_v[rows, :] = (cot[rows, :].astype(F32) + b).astype(BF16)
    grad_copy = pltpu.make_async_copy(grad_v, grad_hbm, lsem.at[1])
    grad_copy.start()

    wg_copies = []
    for h in range(HALVES):
        wait_recv(wg.at[h, pl.ds(0, nh)], GC + h)
        wg_copies.append(
            pltpu.make_async_copy(wg.at[h], wg_hbm.at[:, :, pl.ds(h * HD, HD)], lsem.at[2 + h])
        )
        wg_copies[h].start()

    for ref, i in ((tok3_hbm, TOK), (gg_s, GG), (gated_s, GATED), (grad_s, GRAD)):
        wait_send(ref.at[pl.ds(0, NB - 1)], i)
    for h in range(HALVES):
        wait_send(p_send.at[h], RA + h)
        wait_send(r_x.at[h], RX + h)
        wait_send(r_y.at[h], RY + h)
        if NZ > 1:
            wait_send(r_z.at[h, pl.ds(0, ZL - 1)], RZ + h)
            wait_send(r_v.at[h, pl.ds(0, ZH - 1)], RV + h)
            wait_send(gz.at[h, pl.ds(0, ZL - 1)], GZ + h)
        wait_send(wg.at[h, pl.ds(0, NY - 1)], GY + h)
        wait_send(wg.at[h, pl.ds(0, (NX - 1) * NY)], GX + h)
        wait_send(wg.at[h, pl.ds(0, nh)], GC + h)
    for copy in (out_copy, grad_copy, *wg_copies):
        copy.wait()


def copy_kernel(n, *refs):
    sources, targets, held, sems = refs[:n], refs[n : 2 * n], refs[2 * n : 3 * n], refs[3 * n]
    parts = []
    for i in range(n):
        step = sources[i].shape[0] // 2
        for j in range(2):
            part = pl.ds(j * step, step)
            loads, stores = sems.at[0, 2 * i + j], sems.at[1, 2 * i + j]
            parts.append(
                (
                    pltpu.make_async_copy(sources[i].at[part], held[i].at[part], loads),
                    pltpu.make_async_copy(held[i].at[part], targets[i].at[part], stores),
                )
            )
    for load, _ in parts:
        load.start()
    for load, store in parts:
        load.wait()
        store.start()
    for _, store in parts:
        store.wait()


def body(tokens, cotangent, w_in, w_out, lengths, page_place):
    nblk = E // PAGE
    nh = nblk // NC
    scale_out = 1.0 / math.sqrt(NZ * NC * NB * ROWS)
    vm = pltpu.VMEM
    scratch = [
        vm((ROWS, D), BF16), vm((ROWS, D), BF16), vm((D, 4 * E), BF16), vm((E, D), BF16),
        vm((2, NB), jnp.int32), vm((NB, NB), jnp.int32),
        vm((NB, PAGE, D), BF16),
        vm((NB, PAGE, E), BF16), vm((NB, PAGE, E), BF16),
        vm((NB, PAGE, E), BF16), vm((NB, PAGE, E), BF16),
        vm((NB, PAGE, D), BF16), vm((NB, PAGE, D), BF16),
        vm((ROWS, D), F32), vm((ROWS, 128), F32), vm((ROWS, D), BF16),
        vm((ROWS, 4 * E), BF16), vm((ROWS, 4 * E), F32), vm((ROWS, ROWS), F32),
        vm((HEADS, ROWS, ROWS), BF16), vm((HEADS, ROWS, ROWS), F32),
        vm((ROWS, E), F32), vm((ROWS, 128), F32), vm((ROWS, E), BF16),
        vm((ROWS, 4 * E), BF16), vm((ROWS, D), BF16),
        vm((ROWS, E), BF16),
        vm((HALVES, nh, PAGE, HD), BF16), vm((HALVES, nh, PAGE, HD), F32),
        vm((HALVES, nh, PAGE, HD), BF16), vm((HALVES, nh, PAGE, HD), BF16),
        vm((HALVES, (NX - 1) * NY, PAGE, HD), BF16),
        vm((HALVES, NY, PAGE, HD), BF16), vm((HALVES, NY - 1, PAGE, HD), BF16),
        vm((HALVES, NP, PAGE, 128), F32), vm((HALVES, ZL, PAGE, 128), F32),
        vm((HALVES, ZH, PAGE, 128), F32),
        vm((HALVES, NP, PAGE, 128), BF16),
        vm((HALVES, nblk, PAGE, HD), BF16),
        vm((ROWS, D), BF16), vm((ROWS, D), BF16),
        pltpu.SemaphoreType.DMA((4 + 9 * HALVES,)), pltpu.SemaphoreType.DMA((4 + 9 * HALVES,)),
        pltpu.SemaphoreType.DMA((8,)),
    ]
    hbm = pl.BlockSpec(memory_space=pltpu.HBM)
    results = pl.pallas_call(
        functools.partial(kernel, scale_out),
        out_shape=(
            jax.ShapeDtypeStruct((ROWS, D), BF16),
            jax.ShapeDtypeStruct((ROWS, D), BF16),
            jax.ShapeDtypeStruct((nblk, PAGE, D), BF16),
        ),
        in_specs=[hbm] * 7,
        out_specs=(hbm, hbm, hbm),
        scratch_shapes=scratch,
        compiler_params=pltpu.CompilerParams(
            collective_id=0, has_side_effects=True, vmem_limit_bytes=60 * 1024 * 1024
        ),
    )(
        tokens.reshape(NB, PAGE, D), tokens, cotangent, w_in, w_out,
        jnp.swapaxes(lengths, 1, 2), page_place,
    )
    output, grad_tokens, weight_grad = pl.pallas_call(
        functools.partial(copy_kernel, len(results)),
        out_shape=tuple(jax.ShapeDtypeStruct(r.shape, r.dtype) for r in results),
        in_specs=[hbm] * len(results),
        out_specs=(hbm,) * len(results),
        scratch_shapes=[pltpu.VMEM(r.shape, r.dtype) for r in results]
        + [pltpu.SemaphoreType.DMA((2, 2 * len(results)))],
        compiler_params=pltpu.CompilerParams(vmem_limit_bytes=60 * 1024 * 1024),
    )(*results)
    return output, grad_tokens, weight_grad.reshape(E, D)


def solution(mesh):
    placed = (P(("grp", "bal"), None), P(("grp", "bal"), None), P(), P(), P(), P())
    return jax.shard_map(
        body,
        mesh=mesh,
        in_specs=placed,
        out_specs=(P(("grp", "bal"), None), P(("grp", "bal"), None), P()),
        check_vma=False,
    )
```
